32 devices in a mesh: gz: 2 (over y), gy: 4 (over x, core), gx: 4 (over z).
Axes of the slice: x: 2, y: 2, z: 4, core: 2. Of those that a mesh axis runs over, the one named last changes fastest.
Arguments:
- labels: int32 [2, 32, 512], P('gz', 'gy', 'gx'), may hold values from 0 to 7
- tissue_tensors: float32 [6, 8], replicated, as said below
- electrodes: int32 [2, 64], replicated, may hold values from 0 to 32767, as said below
- initial: float32 [64, 2, 32, 512], P(None, 'gz', 'gy', 'gx'), may hold values from -4 to 4
Outputs:
- solution: float32 [64, 2, 32, 512], P(None, 'gz', 'gy', 'gx')
- residual: float32 [64, 2, 32, 512], P(None, 'gz', 'gy', 'gx')
The draws below stay inside these ranges and needn't reach their ends.
Inputs may be any that keep to these rules, and one draw needn't show every extreme that they name: `tissue_tensors`: the tensors are symmetric and positive definite: each off-diagonal component is at most 0.3 times the geometric mean of its two diagonal components. `electrodes`: all 128 voxel indices are distinct; voxel (z, y, x) has index (z * 32 + y) * 512 + x.
All inputs are finite; a program needn't handle non-finite values.
Results may differ from the reference program's by a relative error of at most 0.0003.
Values sent between devices are 32-bit elements; how exact they have to be, the bound alone decides.
A program may use at most 64 MiB of HBM per device.

```python
import math
import jax
import jax.numpy as jnp
from jax import lax

LEADS = 64
TISSUES = 8
ITERS = 2
NZ = 2
NY = 32
NX = 512


def draw_tissue_tensors(key, part):
    first_key, second_key = jax.random.split(key)
    diagonal = jnp.exp(jax.random.uniform(first_key, (3, TISSUES), jnp.float32, jnp.log(0.2), jnp.log(2.0)))
    spread = jax.random.uniform(second_key, (3, TISSUES), jnp.float32, -1.0, 1.0)
    coupling_xy = 0.3 * spread[0] * jnp.sqrt(diagonal[0] * diagonal[1])
    coupling_xz = 0.3 * spread[1] * jnp.sqrt(diagonal[0] * diagonal[2])
    coupling_yz = 0.3 * spread[2] * jnp.sqrt(diagonal[1] * diagonal[2])
    return jnp.concatenate([diagonal, jnp.stack([coupling_xy, coupling_xz, coupling_yz])], axis=0).astype(jnp.float32)


def draw_electrodes(key, part):
    first_key, second_key = jax.random.split(key)
    count_all = 2 * LEADS
    stratum = NZ * NY * NX // count_all
    offsets = jax.random.randint(first_key, (count_all,), 0, stratum, jnp.int32)
    shuffle = jax.random.permutation(second_key, jnp.arange(count_all, dtype=jnp.int32))
    return (shuffle * stratum + offsets).reshape(2, LEADS).astype(jnp.int32)


def draw_initial(key, part):
    phase_key, freq_key, noise_key = jax.random.split(jax.random.fold_in(key, 7), 3)
    shape = (LEADS, NZ, NY, NX)
    phases = jax.random.uniform(phase_key, (3, LEADS), jnp.float32, -math.pi, math.pi)
    freqs = jax.random.uniform(freq_key, (3, LEADS), jnp.float32, 0.5, 2.0)
    depth = (lax.broadcasted_iota(jnp.float32, (1, NZ, 1, 1), 1) + 0.5) / NZ
    rows = (lax.broadcasted_iota(jnp.float32, (1, 1, NY, 1), 2) + 0.5) / NY
    cols = (lax.broadcasted_iota(jnp.float32, (1, 1, 1, NX), 3) + 0.5) / NX

    def wave(index, coord):
        return 2.0 * math.pi * freqs[index][:, None, None, None] * coord + phases[index][:, None, None, None]
    smooth = jnp.sin(wave(0, depth)) * jnp.cos(wave(1, rows)) + jnp.sin(wave(2, cols))
    noise = jnp.clip(jax.random.normal(noise_key, shape, jnp.float32), -4.0, 4.0)
    value = smooth + 0.5 * noise
    return value.astype(jnp.float32)


def with_ends(array, rng, smallest, top_value):
    longest = array.shape.index(max(array.shape))
    spots = []
    for shift in (0, 1):
        where = [jax.random.randint(jax.random.fold_in(rng, axis), (), 0, length) for axis, length in enumerate(array.shape)]
        where[longest] = (where[longest] + shift) % array.shape[longest]
        spots.append(tuple(where))
    return array.at[spots[0]].set(smallest).at[spots[1]].set(top_value)


def setup_inputs(seed: int = 0) -> dict:
    splits = jax.random.split(jax.random.key(seed), 5)
    return {
        "labels": with_ends(jax.random.randint(splits[0], (NZ, NY, NX), 0, TISSUES), jax.random.fold_in(splits[0], 1), 0, TISSUES - 1).astype(jnp.int32),
        "tissue_tensors": draw_tissue_tensors(jax.random.fold_in(splits[4], 71), 0),
        "electrodes": draw_electrodes(jax.random.fold_in(splits[4], 71), 0),
        "initial": draw_initial(jax.random.fold_in(splits[4], 71), 0),
    }


def tensor_lookup(labels, table):
    result = jnp.zeros((6,) + labels.shape, jnp.float32)
    for tissue in range(table.shape[1]):
        result = result + jnp.where(labels[None] == tissue, table[:, tissue][:, None, None, None], jnp.float32(0.0))
    return result

def flux_terms(tensor, grad_x, grad_y, grad_z):
    flux_x = tensor[0] * grad_x + tensor[3] * grad_y + tensor[4] * grad_z
    flux_y = tensor[3] * grad_x + tensor[1] * grad_y + tensor[5] * grad_z
    flux_z = tensor[4] * grad_x + tensor[5] * grad_y + tensor[2] * grad_z
    return (flux_x, flux_y, flux_z)

def operate_block(group, tensor_padded):
    padded = jnp.pad(group, ((0, 0), (1, 1), (1, 1), (1, 1)))
    centre = padded[:, :-1, :-1, :-1]
    grad_z = padded[:, 1:, :-1, :-1] - centre
    grad_y = padded[:, :-1, 1:, :-1] - centre
    grad_x = padded[:, :-1, :-1, 1:] - centre
    tensor_box = tensor_padded[:, :-1, :-1, :-1]
    flux_x, flux_y, flux_z = flux_terms(tensor_box, grad_x, grad_y, grad_z)
    return flux_z[:, :-1, 1:, 1:] - flux_z[:, 1:, 1:, 1:] + (flux_y[:, 1:, :-1, 1:] - flux_y[:, 1:, 1:, 1:]) + (flux_x[:, 1:, 1:, :-1] - flux_x[:, 1:, 1:, 1:])

def gram_of(first, second):
    leads = first.shape[0]
    return lax.dot_general(first.reshape(leads, -1).astype(jnp.float32), second.reshape(leads, -1).astype(jnp.float32), (((1,), (1,)), ((), ())), precision=lax.Precision.HIGHEST, preferred_element_type=jnp.float32)

def combine_rows(coef, field):
    leads = field.shape[0]
    return jnp.dot(coef.T.astype(jnp.float32), field.reshape(leads, -1).astype(jnp.float32), precision=lax.Precision.HIGHEST, preferred_element_type=jnp.float32).reshape(field.shape)

def factor_solve(matrix, target):
    factor = jnp.linalg.cholesky(matrix)
    halfway = lax.linalg.triangular_solve(factor, target, left_side=True, lower=True)
    return lax.linalg.triangular_solve(factor, halfway, left_side=True, lower=True, transpose_a=True)

def reference(labels, tissue_tensors, electrodes, initial):
    shape = labels.shape
    depth_ids = lax.broadcasted_iota(jnp.int32, shape, 0)
    row_ids = lax.broadcasted_iota(jnp.int32, shape, 1)
    col_ids = lax.broadcasted_iota(jnp.int32, shape, 2)
    voxel_id = (depth_ids * NY + row_ids) * NX + col_ids
    sources = (voxel_id[None] == electrodes[0][:, None, None, None]).astype(jnp.float32) - (voxel_id[None] == electrodes[1][:, None, None, None]).astype(jnp.float32)
    tensor = tensor_lookup(labels, tissue_tensors)
    tensor_padded = jnp.pad(tensor, ((0, 0), (1, 1), (1, 1), (1, 1)))

    def operate(field):
        groups = field.reshape((LEADS // 8, 8) + shape)
        return lax.map(lambda group: operate_block(group, tensor_padded), groups).reshape(field.shape)
    solution = initial
    residual = sources - operate(initial)
    direction = residual
    rr_now = gram_of(residual, residual)
    for iteration in range(ITERS):
        image = operate(direction)
        curve = gram_of(direction, image)
        step_coef = factor_solve(curve, rr_now)
        solution = solution + combine_rows(step_coef, direction)
        residual = residual - combine_rows(step_coef, image)
        if iteration + 1 < ITERS:
            rr_next = gram_of(residual, residual)
            beta_coef = factor_solve(rr_now, rr_next)
            direction = residual + combine_rows(beta_coef, direction)
            rr_now = rr_next
    return (solution, residual)
```

```python
import jax
import jax.numpy as jnp
from jax import lax
from jax.experimental import pallas as pl
from jax.experimental.pallas import tpu as pltpu
from jax.sharding import PartitionSpec as P

MESH = pl.DeviceIdType.MESH
HIGH = lax.Precision.HIGHEST
DEPTH = 3


def nt_dot(a, b):
    return lax.dot_general(
        a, b, (((1,), (1,)), ((), ())), precision=HIGH, preferred_element_type=jnp.float32
    )


def nn_dot(a, b):
    return lax.dot_general(
        a, b, (((1,), (0,)), ((), ())), precision=HIGH, preferred_element_type=jnp.float32
    )


def make_krylov(nz, ny, nx, leads, rows, cols):
    windowed = nz > DEPTH + 1
    layers = 2 * DEPTH + 1 if windowed else nz
    lead8 = leads + 8
    ext = rows + 2 * DEPTH
    top = DEPTH + rows
    if windowed:
        offsets = [d for d in range(-DEPTH, DEPTH + 1) if d]
    else:
        offsets = list(range(1, nz))
    noff = len(offsets)
    plane = nz * ny
    size = 2 * leads
    share = size // plane

    def kernel(
        table, labels, electrodes, field, base_out, gram_out,
        xe, re, qe, coef, inside, elec, xs, xr, gs, rs, zs,
        zsend, zrecv, ysend, yrecv, xsend, xrecv, asend, arecv,
    ):
        z, y, x = lax.axis_index("gz"), lax.axis_index("gy"), lax.axis_index("gx")
        me = z * ny + y
        own = DEPTH if windowed else z
        first = z - DEPTH if windowed else 0

        def plane_peer(k):
            peer = lax.rem(me + k, plane)
            return peer, {"gz": peer // ny, "gy": lax.rem(peer, ny)}

        barrier = pltpu.get_barrier_semaphore()
        for k in range(1, plane):
            pl.semaphore_signal(
                barrier, inc=1, device_id=plane_peer(k)[1], device_id_type=MESH
            )
        for k in range(1, nx):
            pl.semaphore_signal(
                barrier, inc=1, device_id={"gx": lax.rem(x + k, nx)}, device_id_type=MESH
            )

        def fill(slot, lo, hi):
            for r in range(lo, hi):
                xe[slot, r, 0:leads, 0:cols] = jnp.zeros((leads, cols), jnp.float32)
                xe[slot, r, leads:lead8, 0:cols] = jnp.full((8, cols), -1.0, jnp.float32)

        if windowed:
            for s in range(layers):

                @pl.when((first + s < 0) | (first + s >= nz))
                def _(s=s):
                    fill(s, 0, ext)

        for s in range(layers):

            @pl.when(y == 0)
            def _(s=s):
                fill(s, 0, DEPTH)

            @pl.when(y == ny - 1)
            def _(s=s):
                fill(s, top, ext)

        for side, edge in ((0, nx - 1), (1, 0)):

            @pl.when(x == edge)
            def _(side=side):
                for s in range(layers):
                    xr[side, s, 0:leads] = jnp.zeros((leads, cols), jnp.float32)
                    xr[side, s, leads:lead8] = jnp.full((8, cols), -1.0, jnp.float32)

        for r in range(rows):
            xe[own, DEPTH + r, 0:leads, 0:cols] = field[pl.ds(r, leads, stride=rows), :]
            xe[own, DEPTH + r, leads:lead8, 0:cols] = jnp.broadcast_to(
                labels[r : r + 1, :].astype(jnp.float32), (8, cols)
            )
        pl.semaphore_wait(barrier, plane - 1 + nx - 1)

        chunks = ((DEPTH, 2 * DEPTH), (top - DEPTH, top), (2 * DEPTH, top - DEPTH))

        def z_plan(i):
            d = offsets[i]
            if windowed:
                return (
                    z + d, DEPTH - d, DEPTH - d,
                    (z + d >= 0) & (z + d < nz), (z - d >= 0) & (z - d < nz),
                )
            return lax.rem(z + d, nz), z, lax.rem(z - d + nz, nz), None, None

        def when(cond, action):
            if cond is None:
                action()
            else:
                pl.when(cond)(action)

        def z_copy(i, c):
            peer, slot, _, _, _ = z_plan(i)
            lo, hi = chunks[c]
            return pltpu.make_async_remote_copy(
                src_ref=xe.at[own, lo:hi, :, 0:cols],
                dst_ref=xe.at[slot, lo:hi, :, 0:cols],
                send_sem=zsend.at[i, c],
                recv_sem=zrecv.at[i, c],
                device_id={"gz": peer},
                device_id_type=MESH,
            )

        def y_copy(i, slot, up):
            src = (top - DEPTH, top) if up else (DEPTH, 2 * DEPTH)
            dst = (0, DEPTH) if up else (top, ext)
            return pltpu.make_async_remote_copy(
                src_ref=xe.at[slot, src[0] : src[1], :, 0:cols],
                dst_ref=xe.at[slot, dst[0] : dst[1], :, 0:cols],
                send_sem=ysend.at[i, up],
                recv_sem=yrecv.at[i, up],
                device_id={"gy": y + 1 if up else y - 1},
                device_id_type=MESH,
            )

        has_low, has_high = y > 0, y < ny - 1

        def y_start(i, slot, up):
            pl.when(has_high if up else has_low)(lambda: y_copy(i, slot, up).start())

        for c in range(3):
            for i in range(noff):
                when(z_plan(i)[3], lambda i=i, c=c: z_copy(i, c).start())
        for up in (0, 1):
            y_start(noff, own, up)

        eye = lax.broadcasted_iota(jnp.int32, (leads, leads), 0) == lax.broadcasted_iota(
            jnp.int32, (leads, leads), 1
        )
        for e in range(2):
            line = electrodes[e : e + 1, :].astype(jnp.float32)
            column = jnp.sum(
                jnp.where(eye, jnp.broadcast_to(line, (leads, leads)), 0.0), axis=1, keepdims=True
            )
            elec[e] = jnp.broadcast_to(column, (leads, 2 * cols))

        for c in range(2):
            for i in range(noff):

                def arrived(i=i, c=c):
                    z_copy(i, c).wait_recv()
                    y_start(i, z_plan(i)[2], c)

                when(z_plan(i)[4], arrived)
        for i in range(noff):
            when(z_plan(i)[4], lambda i=i: z_copy(i, 2).wait_recv())

        def y_wait(i, slot, up):
            pl.when(has_high if up else has_low)(lambda: y_copy(i, slot, up).wait_send())
            pl.when(has_low if up else has_high)(lambda: y_copy(i, slot, up).wait_recv())

        for up in (0, 1):
            y_wait(noff, own, up)
            for i in range(noff):
                when(z_plan(i)[4], lambda i=i, up=up: y_wait(i, z_plan(i)[2], up))
        for c in range(3):
            for i in range(noff):
                when(z_plan(i)[3], lambda i=i, c=c: z_copy(i, c).wait_send())

        def group(c):
            return pl.ds(pl.multiple_of(c * 8, 8), 8)

        lane = lax.broadcasted_iota(jnp.int32, (8, cols), 1)

        def pack(c, _):
            for s in range(layers):
                total = jnp.zeros((8, cols), jnp.float32)
                for r in range(ext):
                    moved = pltpu.roll(xe[s, r, group(c), 0:cols], 8 * r, axis=1) if r else xe[
                        s, r, group(c), 0:cols
                    ]
                    shifted = lane + DEPTH if r == 0 else lane - (8 * r - DEPTH)
                    keep = (shifted >= 0) & (shifted < 2 * DEPTH)
                    if r == 0:
                        keep = (lane < DEPTH) | (lane >= cols - DEPTH)
                    total = jnp.where(keep, moved, total)
                xs[s, group(c), :] = total
            return 0

        lax.fori_loop(0, lead8 // 8, pack, 0)

        def x_copy(side):
            return pltpu.make_async_remote_copy(
                src_ref=xs,
                dst_ref=xr.at[side],
                send_sem=xsend.at[side],
                recv_sem=xrecv.at[side],
                device_id={"gx": x + 1 if side else x - 1},
                device_id_type=MESH,
            )

        sends = (x > 0, x < nx - 1)
        for side in (0, 1):
            pl.when(sends[side])(lambda side=side: x_copy(side).start())
        for side in (0, 1):
            pl.when(sends[side])(lambda side=side: x_copy(side).wait_send())
            pl.when(sends[1 - side])(lambda side=side: x_copy(side).wait_recv())

        near = (lane & 7) < 4
        rim = (lane < DEPTH) | (lane >= cols - DEPTH)

        def unpack(c, _):
            outside = jnp.where(c == leads // 8, -1.0, 0.0)
            for s in range(layers):
                both = jnp.where(near, xr[0, s, group(c), :], xr[1, s, group(c), :])
                for r in range(ext):
                    moved = pltpu.roll(both, cols - 8 * r, axis=1) if r else both
                    xe[s, r, group(c), cols : 2 * cols] = jnp.where(rim, moved, outside)
            return 0

        lax.fori_loop(0, lead8 // 8, unpack, 0)

        values = [[table[i, t] for t in range(table.shape[1])] for i in range(6)]

        def lookup(r, _):
            for s in range(layers):
                label = xe[s, r, leads:lead8, :]
                parts = [jnp.zeros(label.shape, jnp.float32)] * 6
                for t in range(table.shape[1]):
                    match = label == float(t)
                    parts = [jnp.where(match, values[i][t], parts[i]) for i in range(6)]
                for i in range(6):
                    coef[i, s, r] = parts[i]
                inside[s, r] = jnp.where(label >= 0.0, 1.0, 0.0)
            return 0

        lax.fori_loop(0, ext, lookup, 0)

        wide = 2 * cols
        lanes = lax.broadcasted_iota(jnp.int32, (8, wide), 1)
        column_id = x * cols + jnp.where(lanes >= cols + cols // 2, lanes - wide, lanes)

        def operate(source, emit, lo, hi, c):
            below_y = [None] * layers
            for r in range(lo - 1, hi):
                here = [source[s, r, group(c), :] for s in range(layers)]
                below_z = None
                for s in range(layers):
                    t = [coef[i, s, r] for i in range(6)]
                    v = here[s]
                    grad_x = pltpu.roll(v, wide - 1, axis=1) - v
                    grad_y = source[s, r + 1, group(c), :] - v
                    grad_z = here[s + 1] - v if s + 1 < layers else -v
                    flux_y = t[3] * grad_x + t[1] * grad_y + t[5] * grad_z
                    if r >= lo:
                        flux_x = t[0] * grad_x + t[3] * grad_y + t[4] * grad_z
                        flux_z = t[4] * grad_x + t[5] * grad_y + t[2] * grad_z
                        total = (below_y[s] - flux_y) + (pltpu.roll(flux_x, 1, axis=1) - flux_x)
                        total = total - flux_z if below_z is None else total + (below_z - flux_z)
                        emit(s, r, c, total * inside[s, r])
                        below_z = flux_z
                    below_y[s] = flux_y

        def emit_r(s, r, c, value):
            row_id = (first + s) * (ny * rows) + y * rows + (r - DEPTH)
            voxel = (row_id * (nx * cols) + column_id).astype(jnp.float32)
            source = jnp.where(elec[0, group(c), :] == voxel, 1.0, 0.0) - jnp.where(
                elec[1, group(c), :] == voxel, 1.0, 0.0
            )
            re[s, r, group(c), :] = source * inside[s, r] - value

        def emit_q(s, r, c, value):
            qe[s, r, group(c), :] = value

        def emit_p(s, r, c, value):
            xe[s, r, group(c), 0:cols] = value[:, 0:cols]

        def loop(source, emit, lo, hi):
            def step(c, _):
                operate(source, emit, lo, hi, c)
                return 0

            lax.fori_loop(0, leads // 8, step, 0)

        loop(xe, emit_r, 1, ext - 1)
        loop(re, emit_q, 2, ext - 2)
        loop(qe, emit_p, 3, ext - 3)
        for r in range(rows):
            at = slice(r * cols, (r + 1) * cols)
            base_out[0:leads, at] = re[own, DEPTH + r, :, 0:cols]
            base_out[leads : 2 * leads, at] = qe[own, DEPTH + r, :, 0:cols]
            base_out[2 * leads : 3 * leads, at] = xe[own, DEPTH + r, 0:leads, 0:cols]
        upper = nt_dot(base_out[0:leads, :], base_out[0 : 2 * leads, :])
        lower = nt_dot(base_out[leads : 2 * leads, :], base_out[leads : 3 * leads, :])
        grams = jnp.concatenate([upper, lower], axis=0)
        for i in range(plane):
            gs[i] = grams[i * share : (i + 1) * share, :]

        def a_copy(phase, k, src, dst, device):
            return pltpu.make_async_remote_copy(
                src_ref=src, dst_ref=dst,
                send_sem=asend.at[phase, k], recv_sem=arecv.at[phase, k],
                device_id=device, device_id_type=MESH,
            )

        def scatter(k):
            peer, device = plane_peer(k)
            return a_copy(0, k, gs.at[peer], rs.at[me], device)

        def along(k):
            return a_copy(1, k, zs.at[x], zs.at[x], {"gx": lax.rem(x + k, nx)})

        def gather(k):
            return a_copy(2, k, gram_out.at[me], gram_out.at[me], plane_peer(k)[1])

        def exchange(copy, count):
            for k in range(1, count):
                copy(k).start()
            for k in range(1, count):
                copy(k).wait()

        rs[me] = gs[me]
        exchange(scatter, plane)
        zs[x] = jnp.sum(rs[...], axis=0)
        exchange(along, nx)
        gram_out[me] = jnp.sum(zs[...], axis=0)
        exchange(gather, plane)

    vmem = pl.BlockSpec(memory_space=pltpu.VMEM)
    f32 = jnp.float32
    group_sems = pltpu.SemaphoreType.DMA((3, max(plane, nx)))
    call = pl.pallas_call(
        kernel,
        out_shape=(
            jax.ShapeDtypeStruct((3 * leads, rows * cols), f32),
            jax.ShapeDtypeStruct((plane, share, size), f32),
        ),
        in_specs=[pl.BlockSpec(memory_space=pltpu.SMEM), vmem, vmem, vmem],
        out_specs=(vmem, vmem),
        scratch_shapes=[
            pltpu.VMEM((layers, ext, lead8, 2 * cols), f32),
            pltpu.VMEM((layers, ext, leads, 2 * cols), f32),
            pltpu.VMEM((layers, ext, leads, 2 * cols), f32),
            pltpu.VMEM((6, layers, ext, 8, 2 * cols), f32),
            pltpu.VMEM((layers, ext, 8, 2 * cols), f32),
            pltpu.VMEM((2, leads, 2 * cols), f32),
            pltpu.VMEM((layers, lead8, cols), f32),
            pltpu.VMEM((2, layers, lead8, cols), f32),
            pltpu.VMEM((plane, share, size), f32),
            pltpu.VMEM((plane, share, size), f32),
            pltpu.VMEM((nx, share, size), f32),
            pltpu.SemaphoreType.DMA((noff, 3)),
            pltpu.SemaphoreType.DMA((noff, 3)),
            pltpu.SemaphoreType.DMA((noff + 1, 2)),
            pltpu.SemaphoreType.DMA((noff + 1, 2)),
            pltpu.SemaphoreType.DMA((2,)),
            pltpu.SemaphoreType.DMA((2,)),
            group_sems,
            group_sems,
        ],
        compiler_params=pltpu.CompilerParams(
            collective_id=0, has_side_effects=True,
            vmem_limit_bytes=(8 + 7 * layers) * 1024 * 1024,
        ),
        name="krylov",
    )
    return call, size


def eliminate(matrix, count):
    row_id = lax.broadcasted_iota(jnp.int32, (8, 1), 0)
    tiles = [matrix[i : i + 8, :] for i in range(0, count, 8)]
    for k in range(count):
        home, row = divmod(k, 8)
        source = tiles[home][row : row + 1, :]
        pivot = source * (1.0 / source[:, k : k + 1])
        tiles = [tile - tile[:, k : k + 1] * pivot if i != home else jnp.where(
            row_id == row, pivot, tile - tile[:, k : k + 1] * pivot
        ) for i, tile in enumerate(tiles)]
    return jnp.concatenate(tiles, axis=0)


def make_combine(leads, rows, cols):
    def kernel(gram, base, field, out, res):
        rr, rq = gram[0:leads, 0:leads], gram[0:leads, leads : 2 * leads]
        qq, qp = gram[leads : 2 * leads, 0:leads], gram[leads : 2 * leads, leads : 2 * leads]
        first = eliminate(jnp.concatenate([rq, rr, qq], axis=1), leads)
        z2, z1 = first[:, leads : 2 * leads], first[:, 2 * leads : 3 * leads]
        schur = jnp.concatenate([qp, rq], axis=1) - nn_dot(qq, jnp.concatenate([z1, z2], axis=1))
        e = eliminate(schur, leads)[:, leads : 2 * leads]
        c = z2 - nn_dot(z1, e)
        mix = jnp.transpose(jnp.concatenate([c, e], axis=0))
        gain = nn_dot(mix, base[0 : 2 * leads, :])
        loss = nn_dot(mix, base[leads : 3 * leads, :])
        for r in range(rows):
            at = slice(r * cols, (r + 1) * cols)
            spread = pl.ds(r, leads, stride=rows)
            out[spread, :] = field[spread, :] + gain[:, at]
            res[spread, :] = base[0:leads, at] - loss[:, at]

    vmem = pl.BlockSpec(memory_space=pltpu.VMEM)
    shape = jax.ShapeDtypeStruct((leads * rows, cols), jnp.float32)
    return pl.pallas_call(
        kernel,
        out_shape=(shape, shape),
        in_specs=[vmem] * 3,
        out_specs=(vmem, vmem),
        compiler_params=pltpu.CompilerParams(vmem_limit_bytes=24 * 1024 * 1024),
        name="combine",
    )


def solution(mesh):
    nz, ny, nx = (mesh.shape[name] for name in ("gz", "gy", "gx"))

    def body(labels, tissue_tensors, electrodes, initial):
        leads, _, rows, cols = initial.shape
        field = initial.reshape(leads * rows, cols)
        krylov, size = make_krylov(nz, ny, nx, leads, rows, cols)
        base, gram = krylov(tissue_tensors, labels.reshape(rows, cols), electrodes, field)
        out, res = make_combine(leads, rows, cols)(gram.reshape(size, size), base, field)
        return out.reshape(initial.shape), res.reshape(initial.shape)

    placed = (P("gz", "gy", "gx"), P(), P(), P(None, "gz", "gy", "gx"))
    return jax.shard_map(
        body,
        mesh=mesh,
        in_specs=placed,
        out_specs=(P(None, "gz", "gy", "gx"), P(None, "gz", "gy", "gx")),
        check_vma=False,
    )
```

```python
import jax
import jax.numpy as jnp
from jax import lax
from jax.experimental import pallas as pl
from jax.experimental.pallas import tpu as pltpu
from jax.sharding import PartitionSpec as P

MESH = pl.DeviceIdType.MESH
HIGH = lax.Precision.HIGHEST
DEPTH = 3


def nt_dot(a, b):
    return lax.dot_general(
        a, b, (((1,), (1,)), ((), ())), precision=HIGH, preferred_element_type=jnp.float32
    )


def nn_dot(a, b):
    return lax.dot_general(
        a, b, (((1,), (0,)), ((), ())), precision=HIGH, preferred_element_type=jnp.float32
    )


def make_krylov(nz, ny, nx, leads, rows, cols, classes):
    windowed = nz > DEPTH + 1
    layers = 2 * DEPTH + 1 if windowed else nz
    lead8 = leads + 8
    ext = rows + 2 * DEPTH
    top = DEPTH + rows
    if windowed:
        offsets = [d for d in range(-DEPTH, DEPTH + 1) if d]
    else:
        offsets = list(range(1, nz))
    noff = len(offsets)
    plane = nz * ny
    size = 2 * leads
    share = size // plane

    def kernel(
        table_hbm, labels_hbm, electrodes_hbm, field_hbm, base_out, gram_out,
        table, labels, electrodes, field, lsem,
        xe, re, qe, coef, inside, elec, xs, xr, gs, rs, zs,
        zsend, zrecv, ysend, yrecv, xsend, xrecv, asend, arecv,
    ):
        z, y, x = lax.axis_index("gz"), lax.axis_index("gy"), lax.axis_index("gx")
        me = z * ny + y
        own = DEPTH if windowed else z
        first = z - DEPTH if windowed else 0

        def plane_peer(k):
            peer = lax.rem(me + k, plane)
            return peer, {"gz": peer // ny, "gy": lax.rem(peer, ny)}

        loads = [
            pltpu.make_async_copy(source, target, lsem.at[i])
            for i, (source, target) in enumerate(
                (
                    (field_hbm, field), (labels_hbm, labels),
                    (electrodes_hbm, electrodes), (table_hbm, table),
                )
            )
        ]
        for load in loads:
            load.start()
        barrier = pltpu.get_barrier_semaphore()
        for k in range(1, plane):
            pl.semaphore_signal(
                barrier, inc=1, device_id=plane_peer(k)[1], device_id_type=MESH
            )
        for k in range(1, nx):
            pl.semaphore_signal(
                barrier, inc=1, device_id={"gx": lax.rem(x + k, nx)}, device_id_type=MESH
            )

        def fill(slot, lo, hi):
            for r in range(lo, hi):
                xe[slot, r, 0:leads, 0:cols] = jnp.zeros((leads, cols), jnp.float32)
                xe[slot, r, leads:lead8, 0:cols] = jnp.full((8, cols), -1.0, jnp.float32)

        if windowed:
            for s in range(layers):

                @pl.when((first + s < 0) | (first + s >= nz))
                def _(s=s):
                    fill(s, 0, ext)

        for s in range(layers):

            @pl.when(y == 0)
            def _(s=s):
                fill(s, 0, DEPTH)

            @pl.when(y == ny - 1)
            def _(s=s):
                fill(s, top, ext)

        for side, edge in ((0, nx - 1), (1, 0)):

            @pl.when(x == edge)
            def _(side=side):
                for s in range(layers):
                    xr[side, s, 0:leads] = jnp.zeros((leads, cols), jnp.float32)
                    xr[side, s, leads:lead8] = jnp.full((8, cols), -1.0, jnp.float32)

        for load in loads:
            load.wait()
        for r in range(rows):
            xe[own, DEPTH + r, 0:leads, 0:cols] = field[pl.ds(r, leads, stride=rows), :]
            xe[own, DEPTH + r, leads:lead8, 0:cols] = jnp.broadcast_to(
                labels[r : r + 1, :].astype(jnp.float32), (8, cols)
            )
        pl.semaphore_wait(barrier, plane - 1 + nx - 1)

        chunks = ((DEPTH, 2 * DEPTH), (top - DEPTH, top), (2 * DEPTH, top - DEPTH))

        def z_plan(i):
            d = offsets[i]
            if windowed:
                return (
                    z + d, DEPTH - d, DEPTH - d,
                    (z + d >= 0) & (z + d < nz), (z - d >= 0) & (z - d < nz),
                )
            return lax.rem(z + d, nz), z, lax.rem(z - d + nz, nz), None, None

        def when(cond, action):
            if cond is None:
                action()
            else:
                pl.when(cond)(action)

        def z_copy(i, c):
            peer, slot, _, _, _ = z_plan(i)
            lo, hi = chunks[c]
            return pltpu.make_async_remote_copy(
                src_ref=xe.at[own, lo:hi, :, 0:cols],
                dst_ref=xe.at[slot, lo:hi, :, 0:cols],
                send_sem=zsend.at[i, c],
                recv_sem=zrecv.at[i, c],
                device_id={"gz": peer},
                device_id_type=MESH,
            )

        def y_copy(i, slot, up):
            src = (top - DEPTH, top) if up else (DEPTH, 2 * DEPTH)
            dst = (0, DEPTH) if up else (top, ext)
            return pltpu.make_async_remote_copy(
                src_ref=xe.at[slot, src[0] : src[1], :, 0:cols],
                dst_ref=xe.at[slot, dst[0] : dst[1], :, 0:cols],
                send_sem=ysend.at[i, up],
                recv_sem=yrecv.at[i, up],
                device_id={"gy": y + 1 if up else y - 1},
                device_id_type=MESH,
            )

        has_low, has_high = y > 0, y < ny - 1

        def y_start(i, slot, up):
            pl.when(has_high if up else has_low)(lambda: y_copy(i, slot, up).start())

        def z_start(c):
            for i in range(noff):
                when(z_plan(i)[3], lambda i=i: z_copy(i, c).start())

        z_start(0)
        z_start(1)
        for up in (0, 1):
            y_start(noff, own, up)

        eye = lax.broadcasted_iota(jnp.int32, (leads, leads), 0) == lax.broadcasted_iota(
            jnp.int32, (leads, leads), 1
        )
        for e in range(2):
            line = electrodes[e : e + 1, :].astype(jnp.float32)
            column = jnp.sum(
                jnp.where(eye, jnp.broadcast_to(line, (leads, leads)), 0.0), axis=1, keepdims=True
            )
            elec[e] = jnp.broadcast_to(column, (leads, 2 * cols))

        for c in range(2):
            for i in range(noff):

                def arrived(i=i, c=c):
                    z_copy(i, c).wait_recv()
                    y_start(i, z_plan(i)[2], c)

                when(z_plan(i)[4], arrived)
            if c == 0:
                z_start(2)
        for i in range(noff):
            when(z_plan(i)[4], lambda i=i: z_copy(i, 2).wait_recv())

        def y_wait(i, slot, up):
            pl.when(has_high if up else has_low)(lambda: y_copy(i, slot, up).wait_send())
            pl.when(has_low if up else has_high)(lambda: y_copy(i, slot, up).wait_recv())

        for up in (0, 1):
            y_wait(noff, own, up)
            for i in range(noff):
                when(z_plan(i)[4], lambda i=i, up=up: y_wait(i, z_plan(i)[2], up))
        for c in range(3):
            for i in range(noff):
                when(z_plan(i)[3], lambda i=i, c=c: z_copy(i, c).wait_send())

        def group(c):
            return pl.ds(pl.multiple_of(c * 8, 8), 8)

        lane = lax.broadcasted_iota(jnp.int32, (8, cols), 1)

        def pack(c, _):
            for s in range(layers):
                total = jnp.zeros((8, cols), jnp.float32)
                for r in range(ext):
                    moved = pltpu.roll(xe[s, r, group(c), 0:cols], 8 * r, axis=1) if r else xe[
                        s, r, group(c), 0:cols
                    ]
                    shifted = lane + DEPTH if r == 0 else lane - (8 * r - DEPTH)
                    keep = (shifted >= 0) & (shifted < 2 * DEPTH)
                    if r == 0:
                        keep = (lane < DEPTH) | (lane >= cols - DEPTH)
                    total = jnp.where(keep, moved, total)
                xs[s, group(c), :] = total
            return 0

        lax.fori_loop(0, lead8 // 8, pack, 0)

        def x_copy(side):
            return pltpu.make_async_remote_copy(
                src_ref=xs,
                dst_ref=xr.at[side],
                send_sem=xsend.at[side],
                recv_sem=xrecv.at[side],
                device_id={"gx": x + 1 if side else x - 1},
                device_id_type=MESH,
            )

        sends = (x > 0, x < nx - 1)
        for side in (0, 1):
            pl.when(sends[side])(lambda side=side: x_copy(side).start())
        for side in (0, 1):
            pl.when(sends[side])(lambda side=side: x_copy(side).wait_send())
            pl.when(sends[1 - side])(lambda side=side: x_copy(side).wait_recv())

        near = (lane & 7) < 4
        rim = (lane < DEPTH) | (lane >= cols - DEPTH)

        def unpack(c, _):
            outside = jnp.where(c == leads // 8, -1.0, 0.0)
            for s in range(layers):
                both = jnp.where(near, xr[0, s, group(c), :], xr[1, s, group(c), :])
                for r in range(ext):
                    moved = pltpu.roll(both, cols - 8 * r, axis=1) if r else both
                    xe[s, r, group(c), cols : 2 * cols] = jnp.where(rim, moved, outside)
            return 0

        lax.fori_loop(0, lead8 // 8, unpack, 0)

        values = [[table[i, t] for t in range(table.shape[1])] for i in range(6)]

        def lookup(r, _):
            for s in range(layers):
                label = xe[s, r, leads:lead8, :]
                parts = [jnp.zeros(label.shape, jnp.float32)] * 6
                for t in range(table.shape[1]):
                    match = label == float(t)
                    parts = [jnp.where(match, values[i][t], parts[i]) for i in range(6)]
                for i in range(6):
                    coef[i, s, r] = parts[i]
                inside[s, r] = jnp.where(label >= 0.0, 1.0, 0.0)
            return 0

        lax.fori_loop(0, ext, lookup, 0)

        wide = 2 * cols
        lanes = lax.broadcasted_iota(jnp.int32, (8, wide), 1)
        column_id = x * cols + jnp.where(lanes >= cols + cols // 2, lanes - wide, lanes)

        def operate(source, emit, lo, hi, c):
            below_y = [None] * layers
            for r in range(lo - 1, hi):
                here = [source[s, r, group(c), :] for s in range(layers)]
                below_z = None
                for s in range(layers):
                    t = [coef[i, s, r] for i in range(6)]
                    v = here[s]
                    grad_x = pltpu.roll(v, wide - 1, axis=1) - v
                    grad_y = source[s, r + 1, group(c), :] - v
                    grad_z = here[s + 1] - v if s + 1 < layers else -v
                    flux_y = t[3] * grad_x + t[1] * grad_y + t[5] * grad_z
                    if r >= lo:
                        flux_x = t[0] * grad_x + t[3] * grad_y + t[4] * grad_z
                        flux_z = t[4] * grad_x + t[5] * grad_y + t[2] * grad_z
                        total = (below_y[s] - flux_y) + (pltpu.roll(flux_x, 1, axis=1) - flux_x)
                        total = total - flux_z if below_z is None else total + (below_z - flux_z)
                        emit(s, r, c, total * inside[s, r])
                        below_z = flux_z
                    below_y[s] = flux_y

        def emit_r(s, r, c, value):
            row_id = (first + s) * (ny * rows) + y * rows + (r - DEPTH)
            voxel = (row_id * (nx * cols) + column_id).astype(jnp.float32)
            source = jnp.where(elec[0, group(c), :] == voxel, 1.0, 0.0) - jnp.where(
                elec[1, group(c), :] == voxel, 1.0, 0.0
            )
            re[s, r, group(c), :] = source * inside[s, r] - value

        def emit_q(s, r, c, value):
            qe[s, r, group(c), :] = value

        def emit_p(s, r, c, value):
            xe[s, r, group(c), 0:cols] = value[:, 0:cols]

        def loop(source, emit, lo, hi):
            def step(c, _):
                operate(source, emit, lo, hi, c)
                return 0

            lax.fori_loop(0, leads // 8, step, 0)

        loop(xe, emit_r, 1, ext - 1)
        loop(re, emit_q, 2, ext - 2)
        loop(qe, emit_p, 3, ext - 3)
        for r in range(rows):
            at = slice(r * cols, (r + 1) * cols)
            base_out[0:leads, at] = re[own, DEPTH + r, :, 0:cols]
            base_out[leads : 2 * leads, at] = qe[own, DEPTH + r, :, 0:cols]
            base_out[2 * leads : 3 * leads, at] = xe[own, DEPTH + r, 0:leads, 0:cols]
        upper = nt_dot(base_out[0:leads, :], base_out[0 : 2 * leads, :])
        lower = nt_dot(base_out[leads : 2 * leads, :], base_out[leads : 3 * leads, :])
        grams = jnp.concatenate([upper, lower], axis=0)
        for i in range(plane):
            gs[i] = grams[i * share : (i + 1) * share, :]

        def a_copy(phase, k, src, dst, device):
            return pltpu.make_async_remote_copy(
                src_ref=src, dst_ref=dst,
                send_sem=asend.at[phase, k], recv_sem=arecv.at[phase, k],
                device_id=device, device_id_type=MESH,
            )

        def scatter(k):
            peer, device = plane_peer(k)
            return a_copy(0, k, gs.at[peer], rs.at[me], device)

        def along(k):
            return a_copy(1, k, zs.at[x], zs.at[x], {"gx": lax.rem(x + k, nx)})

        def gather(k):
            return a_copy(2, k, gram_out.at[me], gram_out.at[me], plane_peer(k)[1])

        def exchange(copy, count):
            for k in range(1, count):
                copy(k).start()
            for k in range(1, count):
                copy(k).wait()

        rs[me] = gs[me]
        exchange(scatter, plane)
        zs[x] = jnp.sum(rs[...], axis=0)
        exchange(along, nx)
        gram_out[me] = jnp.sum(zs[...], axis=0)
        exchange(gather, plane)

    vmem = pl.BlockSpec(memory_space=pltpu.VMEM)
    f32 = jnp.float32
    group_sems = pltpu.SemaphoreType.DMA((3, max(plane, nx)))
    call = pl.pallas_call(
        kernel,
        out_shape=(
            jax.ShapeDtypeStruct((3 * leads, rows * cols), f32),
            jax.ShapeDtypeStruct((plane, share, size), f32),
        ),
        in_specs=[pl.BlockSpec(memory_space=pltpu.HBM)] * 4,
        out_specs=(vmem, vmem),
        scratch_shapes=[
            pltpu.SMEM((6, classes), f32),
            pltpu.VMEM((rows, cols), jnp.int32),
            pltpu.VMEM((2, leads), jnp.int32),
            pltpu.VMEM((leads * rows, cols), f32),
            pltpu.SemaphoreType.DMA((4,)),
            pltpu.VMEM((layers, ext, lead8, 2 * cols), f32),
            pltpu.VMEM((layers, ext, leads, 2 * cols), f32),
            pltpu.VMEM((layers, ext, leads, 2 * cols), f32),
            pltpu.VMEM((6, layers, ext, 8, 2 * cols), f32),
            pltpu.VMEM((layers, ext, 8, 2 * cols), f32),
            pltpu.VMEM((2, leads, 2 * cols), f32),
            pltpu.VMEM((layers, lead8, cols), f32),
            pltpu.VMEM((2, layers, lead8, cols), f32),
            pltpu.VMEM((plane, share, size), f32),
            pltpu.VMEM((plane, share, size), f32),
            pltpu.VMEM((nx, share, size), f32),
            pltpu.SemaphoreType.DMA((noff, 3)),
            pltpu.SemaphoreType.DMA((noff, 3)),
            pltpu.SemaphoreType.DMA((noff + 1, 2)),
            pltpu.SemaphoreType.DMA((noff + 1, 2)),
            pltpu.SemaphoreType.DMA((2,)),
            pltpu.SemaphoreType.DMA((2,)),
            group_sems,
            group_sems,
        ],
        compiler_params=pltpu.CompilerParams(
            collective_id=0, has_side_effects=True,
            vmem_limit_bytes=(8 + 7 * layers) * 1024 * 1024,
        ),
        name="krylov",
    )
    return call, size


def eliminate(matrix, count):
    row_id = lax.broadcasted_iota(jnp.int32, (8, 1), 0)
    matrix = matrix * (1.0 / matrix[0:1, 0:1])
    tiles = [matrix[i : i + 8, :] for i in range(0, count, 8)]
    for k in range(0, count, 2):
        home, row = divmod(k, 8)
        one, two = tiles[home][row : row + 1, :], tiles[home][row + 1 : row + 2, :]
        left = [jnp.broadcast_to(tile[:, k : k + 1], tile.shape) for tile in tiles]
        right = [jnp.broadcast_to(tile[:, k + 1 : k + 2], tile.shape) for tile in tiles]
        p11, p21 = left[home][row : row + 1, :], left[home][row + 1 : row + 2, :]
        p12, p22 = right[home][row : row + 1, :], right[home][row + 1 : row + 2, :]
        inverse = 1.0 / (p11 * p22 - p12 * p21)
        first = (p22 * inverse) * one - (p12 * inverse) * two
        second = (p11 * inverse) * two - (p21 * inverse) * one
        tiles = [
            tile - left[i] * first - right[i] * second for i, tile in enumerate(tiles)
        ]
        tiles[home] = jnp.where(
            row_id == row, first, jnp.where(row_id == row + 1, second, tiles[home])
        )
    return jnp.concatenate(tiles, axis=0)


def make_combine(leads, rows, cols):
    def kernel(gram, base, field, out, res):
        rr, rq = gram[0:leads, 0:leads], gram[0:leads, leads : 2 * leads]
        qq, qp = gram[leads : 2 * leads, 0:leads], gram[leads : 2 * leads, leads : 2 * leads]
        first = eliminate(jnp.concatenate([rq, rr, qq], axis=1), leads)
        z2, z1 = first[:, leads : 2 * leads], first[:, 2 * leads : 3 * leads]
        schur = jnp.concatenate([qp, rq], axis=1) - nn_dot(qq, jnp.concatenate([z1, z2], axis=1))
        e = eliminate(schur, leads)[:, leads : 2 * leads]
        c = z2 - nn_dot(z1, e)
        mix = jnp.transpose(jnp.concatenate([c, e], axis=0))
        gain = nn_dot(mix, base[0 : 2 * leads, :])
        loss = nn_dot(mix, base[leads : 3 * leads, :])
        for r in range(rows):
            at = slice(r * cols, (r + 1) * cols)
            spread = pl.ds(r, leads, stride=rows)
            out[spread, :] = field[spread, :] + gain[:, at]
            res[spread, :] = base[0:leads, at] - loss[:, at]

    vmem = pl.BlockSpec(memory_space=pltpu.VMEM)
    shape = jax.ShapeDtypeStruct((leads * rows, cols), jnp.float32)
    return pl.pallas_call(
        kernel,
        out_shape=(shape, shape),
        in_specs=[vmem] * 3,
        out_specs=(vmem, vmem),
        compiler_params=pltpu.CompilerParams(vmem_limit_bytes=24 * 1024 * 1024),
        name="combine",
    )


def solution(mesh):
    nz, ny, nx = (mesh.shape[name] for name in ("gz", "gy", "gx"))

    def body(labels, tissue_tensors, electrodes, initial):
        leads, _, rows, cols = initial.shape
        field = initial.reshape(leads * rows, cols)
        krylov, size = make_krylov(
            nz, ny, nx, leads, rows, cols, tissue_tensors.shape[1]
        )
        base, gram = krylov(tissue_tensors, labels.reshape(rows, cols), electrodes, field)
        out, res = make_combine(leads, rows, cols)(gram.reshape(size, size), base, field)
        return out.reshape(initial.shape), res.reshape(initial.shape)

    placed = (P("gz", "gy", "gx"), P(), P(), P(None, "gz", "gy", "gx"))
    return jax.shard_map(
        body,
        mesh=mesh,
        in_specs=placed,
        out_specs=(P(None, "gz", "gy", "gx"), P(None, "gz", "gy", "gx")),
        check_vma=False,
    )
```

```python
import jax
import jax.numpy as jnp
from jax import lax
from jax.experimental import pallas as pl
from jax.experimental.pallas import tpu as pltpu
from jax.sharding import PartitionSpec as P

MESH = pl.DeviceIdType.MESH
HIGH = lax.Precision.HIGHEST
DEPTH = 3


def nt_dot(a, b):
    return lax.dot_general(
        a, b, (((1,), (1,)), ((), ())), precision=HIGH, preferred_element_type=jnp.float32
    )


def nn_dot(a, b):
    return lax.dot_general(
        a, b, (((1,), (0,)), ((), ())), precision=HIGH, preferred_element_type=jnp.float32
    )


def make_krylov(nz, ny, nx, leads, rows, cols, classes):
    windowed = nz > DEPTH + 1
    layers = 2 * DEPTH + 1 if windowed else nz
    lead8 = leads + 8
    ext = rows + 2 * DEPTH
    top = DEPTH + rows
    if windowed:
        offsets = [d for d in range(-DEPTH, DEPTH + 1) if d]
    else:
        offsets = list(range(1, nz))
    noff = len(offsets)
    plane = nz * ny
    size = 2 * leads
    share = size // plane

    def kernel(
        table_hbm, labels_hbm, electrodes_hbm, field_hbm, base_out, gram_out,
        table, labels, electrodes, field, lsem,
        xe, re, qe, coef, inside, elec, xs, xr, gs, rs, zs,
        zsend, zrecv, ysend, yrecv, xsend, xrecv, asend, arecv,
    ):
        z, y, x = lax.axis_index("gz"), lax.axis_index("gy"), lax.axis_index("gx")
        me = z * ny + y
        own = DEPTH if windowed else z
        first = z - DEPTH if windowed else 0

        def plane_peer(k):
            peer = lax.rem(me + k, plane)
            return peer, {"gz": peer // ny, "gy": lax.rem(peer, ny)}

        loads = [
            pltpu.make_async_copy(source, target, lsem.at[i])
            for i, (source, target) in enumerate(
                (
                    (field_hbm, field), (labels_hbm, labels),
                    (electrodes_hbm, electrodes), (table_hbm, table),
                )
            )
        ]
        for load in loads:
            load.start()
        barrier = pltpu.get_barrier_semaphore()
        for k in range(1, plane):
            pl.semaphore_signal(
                barrier, inc=1, device_id=plane_peer(k)[1], device_id_type=MESH
            )
        for k in range(1, nx):
            pl.semaphore_signal(
                barrier, inc=1, device_id={"gx": lax.rem(x + k, nx)}, device_id_type=MESH
            )

        def fill(slot, lo, hi):
            for r in range(lo, hi):
                xe[slot, r, 0:leads, 0:cols] = jnp.zeros((leads, cols), jnp.float32)
                xe[slot, r, leads:lead8, 0:cols] = jnp.full((8, cols), -1.0, jnp.float32)

        if windowed:
            for s in range(layers):

                @pl.when((first + s < 0) | (first + s >= nz))
                def _(s=s):
                    fill(s, 0, ext)

        for s in range(layers):

            @pl.when(y == 0)
            def _(s=s):
                fill(s, 0, DEPTH)

            @pl.when(y == ny - 1)
            def _(s=s):
                fill(s, top, ext)

        for side, edge in ((0, nx - 1), (1, 0)):

            @pl.when(x == edge)
            def _(side=side):
                for s in range(layers):
                    xr[side, s, 0:leads] = jnp.zeros((leads, cols), jnp.float32)
                    xr[side, s, leads:lead8] = jnp.full((8, cols), -1.0, jnp.float32)

        for load in loads:
            load.wait()
        for r in range(rows):
            xe[own, DEPTH + r, 0:leads, 0:cols] = field[pl.ds(r, leads, stride=rows), :]
            xe[own, DEPTH + r, leads:lead8, 0:cols] = jnp.broadcast_to(
                labels[r : r + 1, :].astype(jnp.float32), (8, cols)
            )
        pl.semaphore_wait(barrier, plane - 1 + nx - 1)

        chunks = ((DEPTH, 2 * DEPTH), (top - DEPTH, top), (2 * DEPTH, top - DEPTH))

        def z_plan(i):
            d = offsets[i]
            if windowed:
                return (
                    z + d, DEPTH - d, DEPTH - d,
                    (z + d >= 0) & (z + d < nz), (z - d >= 0) & (z - d < nz),
                )
            return lax.rem(z + d, nz), z, lax.rem(z - d + nz, nz), None, None

        def when(cond, action):
            if cond is None:
                action()
            else:
                pl.when(cond)(action)

        def z_copy(i, c):
            peer, slot, _, _, _ = z_plan(i)
            lo, hi = chunks[c]
            return pltpu.make_async_remote_copy(
                src_ref=xe.at[own, lo:hi, :, 0:cols],
                dst_ref=xe.at[slot, lo:hi, :, 0:cols],
                send_sem=zsend.at[i, c],
                recv_sem=zrecv.at[i, c],
                device_id={"gz": peer},
                device_id_type=MESH,
            )

        def y_copy(i, slot, up):
            src = (top - DEPTH, top) if up else (DEPTH, 2 * DEPTH)
            dst = (0, DEPTH) if up else (top, ext)
            return pltpu.make_async_remote_copy(
                src_ref=xe.at[slot, src[0] : src[1], :, 0:cols],
                dst_ref=xe.at[slot, dst[0] : dst[1], :, 0:cols],
                send_sem=ysend.at[i, up],
                recv_sem=yrecv.at[i, up],
                device_id={"gy": y + 1 if up else y - 1},
                device_id_type=MESH,
            )

        has_low, has_high = y > 0, y < ny - 1

        def y_start(i, slot, up):
            pl.when(has_high if up else has_low)(lambda: y_copy(i, slot, up).start())

        def z_start(c):
            for i in range(noff):
                when(z_plan(i)[3], lambda i=i: z_copy(i, c).start())

        z_start(0)
        z_start(1)
        for up in (0, 1):
            y_start(noff, own, up)

        eye = lax.broadcasted_iota(jnp.int32, (leads, leads), 0) == lax.broadcasted_iota(
            jnp.int32, (leads, leads), 1
        )
        for e in range(2):
            line = electrodes[e : e + 1, :].astype(jnp.float32)
            column = jnp.sum(
                jnp.where(eye, jnp.broadcast_to(line, (leads, leads)), 0.0), axis=1, keepdims=True
            )
            elec[e] = jnp.broadcast_to(column, (leads, 2 * cols))

        def y_wait(i, slot, up):
            pl.when(has_high if up else has_low)(lambda: y_copy(i, slot, up).wait_send())
            pl.when(has_low if up else has_high)(lambda: y_copy(i, slot, up).wait_recv())

        def group(c):
            return pl.ds(pl.multiple_of(c * 8, 8), 8)

        lane = lax.broadcasted_iota(jnp.int32, (8, cols), 1)

        def pack(c, s):
            total = jnp.zeros((8, cols), jnp.float32)
            for r in range(ext):
                moved = pltpu.roll(xe[s, r, group(c), 0:cols], 8 * r, axis=1) if r else xe[
                    s, r, group(c), 0:cols
                ]
                shifted = lane + DEPTH if r == 0 else lane - (8 * r - DEPTH)
                keep = (shifted >= 0) & (shifted < 2 * DEPTH)
                if r == 0:
                    keep = (lane < DEPTH) | (lane >= cols - DEPTH)
                total = jnp.where(keep, moved, total)
            xs[s, group(c), :] = total
            return s

        def x_copy(side, i, slot):
            return pltpu.make_async_remote_copy(
                src_ref=xs.at[slot],
                dst_ref=xr.at[side, slot],
                send_sem=xsend.at[side, i],
                recv_sem=xrecv.at[side, i],
                device_id={"gx": x + 1 if side else x - 1},
                device_id_type=MESH,
            )

        sends = (x > 0, x < nx - 1)

        def x_start(i, slot):
            lax.fori_loop(0, lead8 // 8, pack, slot)
            for side in (0, 1):
                pl.when(sends[side])(lambda side=side: x_copy(side, i, slot).start())

        def x_wait(i, slot):
            for side in (0, 1):
                pl.when(sends[side])(lambda side=side: x_copy(side, i, slot).wait_send())
                pl.when(sends[1 - side])(lambda side=side: x_copy(side, i, slot).wait_recv())

        for up in (0, 1):
            y_wait(noff, own, up)
        x_start(noff, own)

        for c in range(2):
            for i in range(noff):

                def arrived(i=i, c=c):
                    z_copy(i, c).wait_recv()
                    y_start(i, z_plan(i)[2], c)

                when(z_plan(i)[4], arrived)
            if c == 0:
                z_start(2)
        for i in range(noff):
            when(z_plan(i)[4], lambda i=i: z_copy(i, 2).wait_recv())

        for up in (0, 1):
            for i in range(noff):
                when(z_plan(i)[4], lambda i=i, up=up: y_wait(i, z_plan(i)[2], up))
        for i in range(noff):
            x_start(i, z_plan(i)[2])
        for c in range(3):
            for i in range(noff):
                when(z_plan(i)[3], lambda i=i, c=c: z_copy(i, c).wait_send())
        x_wait(noff, own)
        for i in range(noff):
            x_wait(i, z_plan(i)[2])

        near = (lane & 7) < 4
        rim = (lane < DEPTH) | (lane >= cols - DEPTH)

        def unpack(c, _):
            outside = jnp.where(c == leads // 8, -1.0, 0.0)
            for s in range(layers):
                both = jnp.where(near, xr[0, s, group(c), :], xr[1, s, group(c), :])
                for r in range(ext):
                    moved = pltpu.roll(both, cols - 8 * r, axis=1) if r else both
                    xe[s, r, group(c), cols : 2 * cols] = jnp.where(rim, moved, outside)
            return 0

        lax.fori_loop(0, lead8 // 8, unpack, 0)

        values = [[table[i, t] for t in range(table.shape[1])] for i in range(6)]

        def lookup(r, _):
            for s in range(layers):
                label = xe[s, r, leads:lead8, :]
                parts = [jnp.zeros(label.shape, jnp.float32)] * 6
                for t in range(table.shape[1]):
                    match = label == float(t)
                    parts = [jnp.where(match, values[i][t], parts[i]) for i in range(6)]
                for i in range(6):
                    coef[i, s, r] = parts[i]
                inside[s, r] = jnp.where(label >= 0.0, 1.0, 0.0)
            return 0

        lax.fori_loop(0, ext, lookup, 0)

        wide = 2 * cols
        lanes = lax.broadcasted_iota(jnp.int32, (8, wide), 1)
        column_id = x * cols + jnp.where(lanes >= cols + cols // 2, lanes - wide, lanes)

        def operate(source, emit, lo, hi, c):
            below_y = [None] * layers
            for r in range(lo - 1, hi):
                here = [source[s, r, group(c), :] for s in range(layers)]
                below_z = None
                for s in range(layers):
                    t = [coef[i, s, r] for i in range(6)]
                    v = here[s]
                    grad_x = pltpu.roll(v, wide - 1, axis=1) - v
                    grad_y = source[s, r + 1, group(c), :] - v
                    grad_z = here[s + 1] - v if s + 1 < layers else -v
                    flux_y = t[3] * grad_x + t[1] * grad_y + t[5] * grad_z
                    if r >= lo:
                        flux_x = t[0] * grad_x + t[3] * grad_y + t[4] * grad_z
                        flux_z = t[4] * grad_x + t[5] * grad_y + t[2] * grad_z
                        total = (below_y[s] - flux_y) + (pltpu.roll(flux_x, 1, axis=1) - flux_x)
                        total = total - flux_z if below_z is None else total + (below_z - flux_z)
                        emit(s, r, c, total * inside[s, r])
                        below_z = flux_z
                    below_y[s] = flux_y

        def emit_r(s, r, c, value):
            row_id = (first + s) * (ny * rows) + y * rows + (r - DEPTH)
            voxel = (row_id * (nx * cols) + column_id).astype(jnp.float32)
            source = jnp.where(elec[0, group(c), :] == voxel, 1.0, 0.0) - jnp.where(
                elec[1, group(c), :] == voxel, 1.0, 0.0
            )
            re[s, r, group(c), :] = source * inside[s, r] - value

        def emit_q(s, r, c, value):
            qe[s, r, group(c), :] = value

        def emit_p(s, r, c, value):
            xe[s, r, group(c), 0:cols] = value[:, 0:cols]

        def loop(source, emit, lo, hi):
            def step(c, _):
                operate(source, emit, lo, hi, c)
                return 0

            lax.fori_loop(0, leads // 8, step, 0)

        loop(xe, emit_r, 1, ext - 1)
        loop(re, emit_q, 2, ext - 2)
        loop(qe, emit_p, 3, ext - 3)
        for r in range(rows):
            at = slice(r * cols, (r + 1) * cols)
            base_out[0:leads, at] = re[own, DEPTH + r, :, 0:cols]
            base_out[leads : 2 * leads, at] = qe[own, DEPTH + r, :, 0:cols]
            base_out[2 * leads : 3 * leads, at] = xe[own, DEPTH + r, 0:leads, 0:cols]
        upper = nt_dot(base_out[0:leads, :], base_out[0 : 2 * leads, :])
        lower = nt_dot(base_out[leads : 2 * leads, :], base_out[leads : 3 * leads, :])
        grams = jnp.concatenate([upper, lower], axis=0)
        for i in range(plane):
            gs[i] = grams[i * share : (i + 1) * share, :]

        def a_copy(phase, k, src, dst, device):
            return pltpu.make_async_remote_copy(
                src_ref=src, dst_ref=dst,
                send_sem=asend.at[phase, k], recv_sem=arecv.at[phase, k],
                device_id=device, device_id_type=MESH,
            )

        def scatter(k):
            peer, device = plane_peer(k)
            return a_copy(0, k, gs.at[peer], rs.at[me], device)

        def along(k):
            return a_copy(1, k, zs.at[x], zs.at[x], {"gx": lax.rem(x + k, nx)})

        def gather(k):
            return a_copy(2, k, gram_out.at[me], gram_out.at[me], plane_peer(k)[1])

        def exchange(copy, count):
            for k in range(1, count):
                copy(k).start()
            for k in range(1, count):
                copy(k).wait()

        rs[me] = gs[me]
        exchange(scatter, plane)
        zs[x] = jnp.sum(rs[...], axis=0)
        exchange(along, nx)
        gram_out[me] = jnp.sum(zs[...], axis=0)
        exchange(gather, plane)

    vmem = pl.BlockSpec(memory_space=pltpu.VMEM)
    f32 = jnp.float32
    group_sems = pltpu.SemaphoreType.DMA((3, max(plane, nx)))
    call = pl.pallas_call(
        kernel,
        out_shape=(
            jax.ShapeDtypeStruct((3 * leads, rows * cols), f32),
            jax.ShapeDtypeStruct((plane, share, size), f32),
        ),
        in_specs=[pl.BlockSpec(memory_space=pltpu.HBM)] * 4,
        out_specs=(vmem, vmem),
        scratch_shapes=[
            pltpu.SMEM((6, classes), f32),
            pltpu.VMEM((rows, cols), jnp.int32),
            pltpu.VMEM((2, leads), jnp.int32),
            pltpu.VMEM((leads * rows, cols), f32),
            pltpu.SemaphoreType.DMA((4,)),
            pltpu.VMEM((layers, ext, lead8, 2 * cols), f32),
            pltpu.VMEM((layers, ext, leads, 2 * cols), f32),
            pltpu.VMEM((layers, ext, leads, 2 * cols), f32),
            pltpu.VMEM((6, layers, ext, 8, 2 * cols), f32),
            pltpu.VMEM((layers, ext, 8, 2 * cols), f32),
            pltpu.VMEM((2, leads, 2 * cols), f32),
            pltpu.VMEM((layers, lead8, cols), f32),
            pltpu.VMEM((2, layers, lead8, cols), f32),
            pltpu.VMEM((plane, share, size), f32),
            pltpu.VMEM((plane, share, size), f32),
            pltpu.VMEM((nx, share, size), f32),
            pltpu.SemaphoreType.DMA((noff, 3)),
            pltpu.SemaphoreType.DMA((noff, 3)),
            pltpu.SemaphoreType.DMA((noff + 1, 2)),
            pltpu.SemaphoreType.DMA((noff + 1, 2)),
            pltpu.SemaphoreType.DMA((2, noff + 1)),
            pltpu.SemaphoreType.DMA((2, noff + 1)),
            group_sems,
            group_sems,
        ],
        compiler_params=pltpu.CompilerParams(
            collective_id=0, has_side_effects=True,
            vmem_limit_bytes=(8 + 7 * layers) * 1024 * 1024,
        ),
        name="krylov",
    )
    return call, size


def eliminate(matrix, count):
    row_id = lax.broadcasted_iota(jnp.int32, (8, 1), 0)
    matrix = matrix * (1.0 / matrix[0:1, 0:1])
    tiles = [matrix[i : i + 8, :] for i in range(0, count, 8)]
    for k in range(0, count, 2):
        home, row = divmod(k, 8)
        one, two = tiles[home][row : row + 1, :], tiles[home][row + 1 : row + 2, :]
        left = [jnp.broadcast_to(tile[:, k : k + 1], tile.shape) for tile in tiles]
        right = [jnp.broadcast_to(tile[:, k + 1 : k + 2], tile.shape) for tile in tiles]
        p11, p21 = left[home][row : row + 1, :], left[home][row + 1 : row + 2, :]
        p12, p22 = right[home][row : row + 1, :], right[home][row + 1 : row + 2, :]
        inverse = 1.0 / (p11 * p22 - p12 * p21)
        first = (p22 * inverse) * one - (p12 * inverse) * two
        second = (p11 * inverse) * two - (p21 * inverse) * one
        tiles = [
            tile - left[i] * first - right[i] * second for i, tile in enumerate(tiles)
        ]
        tiles[home] = jnp.where(
            row_id == row, first, jnp.where(row_id == row + 1, second, tiles[home])
        )
    return jnp.concatenate(tiles, axis=0)


def make_combine(leads, rows, cols):
    def kernel(gram, base, field, out, res):
        rr, rq = gram[0:leads, 0:leads], gram[0:leads, leads : 2 * leads]
        qq, qp = gram[leads : 2 * leads, 0:leads], gram[leads : 2 * leads, leads : 2 * leads]
        first = eliminate(jnp.concatenate([rq, rr, qq], axis=1), leads)
        z2, z1 = first[:, leads : 2 * leads], first[:, 2 * leads : 3 * leads]
        schur = jnp.concatenate([qp, rq], axis=1) - nn_dot(qq, jnp.concatenate([z1, z2], axis=1))
        e = eliminate(schur, leads)[:, leads : 2 * leads]
        c = z2 - nn_dot(z1, e)
        mix = jnp.transpose(jnp.concatenate([c, e], axis=0))
        gain = nn_dot(mix, base[0 : 2 * leads, :])
        loss = nn_dot(mix, base[leads : 3 * leads, :])
        for r in range(rows):
            at = slice(r * cols, (r + 1) * cols)
            spread = pl.ds(r, leads, stride=rows)
            out[spread, :] = field[spread, :] + gain[:, at]
            res[spread, :] = base[0:leads, at] - loss[:, at]

    vmem = pl.BlockSpec(memory_space=pltpu.VMEM)
    shape = jax.ShapeDtypeStruct((leads * rows, cols), jnp.float32)
    return pl.pallas_call(
        kernel,
        out_shape=(shape, shape),
        in_specs=[vmem] * 3,
        out_specs=(vmem, vmem),
        compiler_params=pltpu.CompilerParams(vmem_limit_bytes=24 * 1024 * 1024),
        name="combine",
    )


def solution(mesh):
    nz, ny, nx = (mesh.shape[name] for name in ("gz", "gy", "gx"))

    def body(labels, tissue_tensors, electrodes, initial):
        leads, _, rows, cols = initial.shape
        field = initial.reshape(leads * rows, cols)
        krylov, size = make_krylov(
            nz, ny, nx, leads, rows, cols, tissue_tensors.shape[1]
        )
        base, gram = krylov(tissue_tensors, labels.reshape(rows, cols), electrodes, field)
        out, res = make_combine(leads, rows, cols)(gram.reshape(size, size), base, field)
        return out.reshape(initial.shape), res.reshape(initial.shape)

    placed = (P("gz", "gy", "gx"), P(), P(), P(None, "gz", "gy", "gx"))
    return jax.shard_map(
        body,
        mesh=mesh,
        in_specs=placed,
        out_specs=(P(None, "gz", "gy", "gx"), P(None, "gz", "gy", "gx")),
        check_vma=False,
    )
```
